128 devices in a mesh: row: 8 (over y, core), col: 16 (over x, z).
Axes of the slice: x: 4, y: 4, z: 4, core: 2. Of those that a mesh axis runs over, the one named last changes fastest.
Arguments:
- activations: bfloat16 [1024, 8192], P('col', 'row')
- out_grads: bfloat16 [1024, 32768], P('row', 'col')
- queries: bfloat16 [4, 8192, 32768], P(None, 'row', 'col'), may hold values from -0.00036621094 to 0.00036621094
- seq_start: int32 [16], replicated, may hold values from 0 to 1008, as said below
- seq_len: int32 [16], replicated, may hold values from 16 to 64, as said below
Outputs:
- scores: float32 [4, 16], replicated
The draws below stay inside these ranges and needn't reach their ends.
Inputs may be any that keep to these rules, and one draw needn't show every extreme that they name: `seq_start`: sequence s lies inside tokens s * 64 to (s + 1) * 64 - 1. `seq_len`: some sequence has exactly 64 tokens and some exactly 16.
All inputs are finite; a program needn't handle non-finite values.
Results may differ from the reference program's by a relative error of at most 0.0003.
Values may be sent and summed in bfloat16 or wider, within the bound.
No kernel may reach another device: no remote copies, remote signals or barrier semaphores. Data moves between devices by JAX's collectives and lax.ppermute only.
A program may use at most 192 MiB of HBM per device.

```python
import jax
import jax.numpy as jnp
from jax import lax

D_IN = 8192
D_OUT = 32768
NQ = 4
NSEQ = 16
TOKENS = 1024
SLOT = 64


def seq_layout(key):
    key_len, key_perm, key_off = jax.random.split(jax.random.fold_in(key, 41), 3)
    least = SLOT // 4
    lengths = jax.random.randint(key_len, (NSEQ,), least, SLOT + 1)
    order = jax.random.permutation(key_perm, NSEQ)
    lengths = lengths.at[order[0]].set(SLOT).at[order[1]].set(least)
    offsets = jax.random.randint(key_off, (NSEQ,), 0, SLOT - lengths + 1)
    starts = jnp.arange(NSEQ, dtype=jnp.int32) * SLOT + offsets
    return (starts.astype(jnp.int32), lengths.astype(jnp.int32))


def scaled_columns(key, rows, columns, factor):
    ramp = jnp.arange(columns, dtype=jnp.float32) / max(columns - 1, 1)
    column_scale = jnp.exp(jnp.log(factor) * ramp)
    key_main = jax.random.fold_in(key, 0)
    values = jax.random.normal(key_main, (rows, columns), jnp.float32)
    values = jnp.clip(values, -6.0, 6.0)
    return values * column_scale[None, :] / jnp.sqrt(factor)


def draw_activations(key, part):
    key = jax.random.fold_in(key, 3)
    factor = 3.0
    return scaled_columns(key, TOKENS, D_IN, factor).astype(jnp.bfloat16)


def draw_out_grads(key, part):
    key = jax.random.fold_in(key, 5)
    factor = 3.0
    return scaled_columns(key, TOKENS, D_OUT, factor).astype(jnp.bfloat16)


def draw_seq_start(key, part):
    starts, lengths = seq_layout(key)
    return starts


def draw_seq_len(key, part):
    starts, lengths = seq_layout(key)
    return lengths


def shard_levels(key, dims, shards, smallest, largest):
    def one(dim, shards_of):
        steps = jax.random.uniform(jax.random.fold_in(jax.random.fold_in(key, 6), dim), (shards_of,), jnp.float32, smallest / len(shards), largest / len(shards))
        return jnp.repeat(jnp.exp(steps), dims[dim] // shards_of).reshape((-1,) + (1,) * (len(dims) - dim - 1))

    factor_of = one(*shards[0])
    for cut in shards[1:]:
        factor_of = factor_of * one(*cut)
    return factor_of


def gaussian(rng, extent, width, limit, shards=(), held_as=jnp.bfloat16):
    level = shard_levels(rng, extent, shards, -0.22, 0.18) if shards else 1.0
    drawn = jax.random.normal(rng, extent, jnp.float32) * width * level
    return jnp.minimum(jnp.maximum(drawn, -limit), limit).astype(held_as)


def setup_inputs(seed: int = 0) -> dict:
    keys = jax.random.split(jax.random.key(seed), 6)
    activations = draw_activations(jax.random.fold_in(keys[5], 71), 0)
    out_grads = draw_out_grads(jax.random.fold_in(keys[5], 71), 0)
    queries = gaussian(keys[2], (NQ, D_IN, D_OUT), (D_IN * D_OUT) ** -0.5, 0.00036621094, ((1, 8), (2, 16)))
    seq_start = draw_seq_start(jax.random.fold_in(keys[5], 71), 0)
    seq_len = draw_seq_len(jax.random.fold_in(keys[5], 71), 0)
    return {"activations": activations, "out_grads": out_grads, "queries": queries, "seq_start": seq_start, "seq_len": seq_len}


def reference(activations, out_grads, queries, seq_start, seq_len):
    slot_size = TOKENS // NSEQ
    positions = jnp.arange(TOKENS, dtype=jnp.int32).reshape(NSEQ, slot_size)
    inside = (positions >= seq_start[:, None]) & (positions < (seq_start + seq_len)[:, None])
    act_slots = activations.reshape(NSEQ, slot_size, D_IN)
    grad_slots = out_grads.reshape(NSEQ, slot_size, D_OUT)

    def per_sequence(inputs):
        act_block, grad_block, inside_block = inputs
        masked = jnp.where(inside_block[:, None], act_block, jnp.zeros_like(act_block))
        grad_tile = jnp.dot(masked.T, grad_block, preferred_element_type=jnp.float32)
        return lax.map(lambda query_one: jnp.sum(query_one.astype(jnp.float32) * grad_tile), queries)

    per_seq = lax.map(per_sequence, (act_slots, grad_slots, inside))
    return per_seq.T
```

```python
import functools

import jax
import jax.numpy as jnp
from jax import lax
from jax.experimental import pallas as pl
from jax.experimental.pallas import tpu as pltpu
from jax.sharding import PartitionSpec as P

NT = (((1,), (1,)), ((), ()))
SLOT = 64
VMEM = pl.BlockSpec(memory_space=pltpu.VMEM)
SMEM = pl.BlockSpec(memory_space=pltpu.SMEM)
ANY = pl.BlockSpec(memory_space=pl.ANY)


def along_y(shift):
    return [(i, ((i // 2 + shift) % 4) * 2 + i % 2) for i in range(8)]


def along_z(shift):
    return [(i, (i // 4) * 4 + (i + shift) % 4) for i in range(16)]


def along_x(shift):
    return [(i, (i + 4 * shift) % 16) for i in range(16)]


OTHER_CORE = [(i, i ^ 1) for i in range(8)]


def first_row(place):
    dy, dcore, row = place
    index = lax.axis_index("row")
    y, core = index // 2, index % 2
    return pl.multiple_of((y + dy) % 4 * 256 + (core + dcore) % 2 * 128 + row, SLOT)


def multiply(places, blocks, rows, query, products, q):
    start = 0
    for block in blocks:
        rows[start : start + block.shape[0], :] = block[...]
        start += block.shape[0]

    result = lax.dot_general(rows[...], query, NT, preferred_element_type=jnp.float32)
    start = 0
    for place, block in zip(places, blocks, strict=True):
        count = block.shape[0]
        products[q, pl.ds(first_row(place), count), :] = result[start : start + count]
        start += count


def first_kernel(places, *refs):
    n = len(places)
    blocks, queries, products, held, rows, sems = refs[:n], refs[n], *refs[n + 1 :]
    copies = [pltpu.make_async_copy(queries.at[q], held.at[q], sems.at[q]) for q in range(queries.shape[0])]
    for copy in copies:
        copy.start()
    for q, copy in enumerate(copies):
        copy.wait()
        multiply(places, blocks, rows, held[q], products, q)


def next_kernel(places, *refs):
    n = len(places)
    blocks, held, _, products, rows = refs[:n], refs[n], *refs[n + 1 :]

    def one_query(q, carry):
        multiply(places, blocks, rows, held[q], products, q)
        return carry

    lax.fori_loop(0, held.shape[0], one_query, 0)


def params(limit):
    return pltpu.CompilerParams(vmem_limit_bytes=limit << 20)


def cost(blocks, queries):
    rows = sum(b.shape[0] for b in blocks)
    return pl.CostEstimate(flops=2 * rows * queries.size, bytes_accessed=2 * queries.size, transcendentals=0)


def first_products(name, places, blocks, queries, tokens):
    nq, width, depth = queries.shape
    rows = sum(b.shape[0] for b in blocks)
    return pl.pallas_call(
        functools.partial(first_kernel, places),
        in_specs=[VMEM] * len(blocks) + [ANY],
        out_specs=[VMEM, VMEM],
        out_shape=[pltpu.VMEM((nq, tokens, width), jnp.float32), pltpu.VMEM(queries.shape, queries.dtype)],
        scratch_shapes=[pltpu.VMEM((rows, depth), jnp.bfloat16), pltpu.SemaphoreType.DMA((nq,))],
        compiler_params=params(8),
        cost_estimate=cost(blocks, queries),
        name=name,
    )(*blocks, queries)


def next_products(name, places, blocks, held, products):
    rows = sum(b.shape[0] for b in blocks)
    n = len(blocks)
    return pl.pallas_call(
        functools.partial(next_kernel, places),
        in_specs=[VMEM] * (n + 2),
        out_specs=VMEM,
        out_shape=pltpu.VMEM(products.shape, products.dtype),
        input_output_aliases={n + 1: 0},
        scratch_shapes=[pltpu.VMEM((rows, held.shape[2]), jnp.bfloat16)],
        compiler_params=params(8),
        cost_estimate=cost(blocks, held),
        name=name,
    )(*blocks, held, products)


def score_kernel(seq_start, seq_len, own, ahead, far, behind, products, out, lanes):
    col = lax.axis_index("col")
    x, z = col // 4, col % 4
    nq = out.shape[0]
    width = products.shape[2]
    position = lax.broadcasted_iota(jnp.int32, (SLOT, 1), 0)
    for dx, block in enumerate((own, ahead, far, behind)):

        def one_slot(dz, carry, dx=dx, block=block):
            slot = (x + dx) % 4 * 4 + (z + dz) % 4
            base = pl.multiple_of(slot * SLOT, SLOT)
            token = position + base
            start = seq_start[slot]
            inside = (token >= start) & (token < start + seq_len[slot])
            totals = [jnp.zeros((SLOT, 128), jnp.float32) for _ in range(nq)]
            for i in range(0, width, 128):
                act = block[dz, :, i : i + 128].astype(jnp.float32)
                for q in range(nq):
                    totals[q] += products[q, pl.ds(base, SLOT), i : i + 128] * act
            for q in range(nq):
                kept = jnp.where(inside, totals[q], 0.0)
                lanes[q, pl.ds(slot, 1), :] = jnp.sum(kept, axis=0, keepdims=True)
            return carry

        lax.fori_loop(0, 4, one_slot, 0)
    ones = jnp.ones((8, 128), jnp.float32)
    for q in range(nq):
        sums = lax.dot_general(ones, lanes[q], NT, precision=lax.Precision.HIGHEST, preferred_element_type=jnp.float32)
        out[q : q + 1, :] = sums[:1, :]


def partial_scores(seq_start, seq_len, acts, products):
    nq = products.shape[0]
    nseq = seq_start.shape[0]
    return pl.pallas_call(
        score_kernel,
        in_specs=[SMEM] * 2 + [VMEM] * 5,
        out_specs=VMEM,
        out_shape=jax.ShapeDtypeStruct((nq, nseq), jnp.float32),
        scratch_shapes=[pltpu.VMEM((nq, nseq, 128), jnp.float32)],
        compiler_params=params(8),
        cost_estimate=pl.CostEstimate(flops=1 << 30, bytes_accessed=4 << 20, transcendentals=0),
        name="scores",
    )(seq_start, seq_len, *acts, products)


def everywhere(value, axis, size):
    copies = jnp.broadcast_to(value[None], (size,) + value.shape)
    return jnp.sum(lax.all_to_all(copies, axis, 0, 0, tiled=True), axis=0)


def on_device(activations, out_grads, queries, seq_start, seq_len):
    half = out_grads.shape[0] // 2
    tokens = SLOT * seq_start.shape[0]

    def to_core(block):
        return lax.ppermute(block, "row", OTHER_CORE)

    def rows_of_z(block):
        parts = [block] + [lax.ppermute(block, "col", along_z(-d)) for d in (1, 2, 3)]
        return jnp.stack(parts)

    from_below = lax.ppermute(out_grads, "row", along_y(1))
    from_above = lax.ppermute(out_grads, "row", along_y(-1))
    products, held = first_products(
        "near", [(0, 0, 0), (0, 1, 0)], [out_grads, to_core(out_grads)], queries, tokens
    )

    far_one = lax.ppermute(activations, "col", along_x(2))
    own = rows_of_z(activations)
    far_act = rows_of_z(far_one)
    ahead = lax.ppermute(own, "col", along_x(-1))
    behind = lax.ppermute(own, "col", along_x(1))

    far_first = lax.ppermute(from_below[:half], "row", along_y(1))
    far_second = lax.ppermute(from_above[half:], "row", along_y(-1))
    products = next_products("mid", [(3, 0, 0), (1, 0, 0)], [from_below, from_above], held, products)
    products = next_products(
        "mid_core", [(3, 1, 0), (1, 1, 0)], [to_core(from_below), to_core(from_above)], held, products
    )
    products = next_products(
        "far",
        [(2, 0, 0), (2, 0, half), (2, 1, 0), (2, 1, half)],
        [far_first, far_second, to_core(far_first), to_core(far_second)],
        held,
        products,
    )
    scores = partial_scores(seq_start, seq_len, [own, ahead, far_act, behind], products)
    scores = everywhere(scores, "row", lax.axis_size("row"))
    return everywhere(scores, "col", lax.axis_size("col"))


def solution(mesh):
    in_specs = (P("col", "row"), P("row", "col"), P(None, "row", "col"), P(), P())
    return jax.shard_map(on_device, mesh=mesh, in_specs=in_specs, out_specs=P(), check_vma=False)
```

```python
import functools

import jax
import jax.numpy as jnp
from jax import lax
from jax.experimental import pallas as pl
from jax.experimental.pallas import tpu as pltpu
from jax.sharding import PartitionSpec as P

NT = (((1,), (1,)), ((), ()))
SLOT = 64
BLOCK = 128
VMEM = pl.BlockSpec(memory_space=pltpu.VMEM)
SMEM = pl.BlockSpec(memory_space=pltpu.SMEM)
HBM = pl.BlockSpec(memory_space=pltpu.HBM)
TOKEN = pltpu.VMEM((8, 128), jnp.float32)
SMALL = pltpu.CompilerParams(vmem_limit_bytes=8 << 20)
WEIGHT = 10


def along_y(shift):
    return [(i, ((i // 2 + shift) % 4) * 2 + i % 2) for i in range(8)]


def along_z(col, shift):
    return col // 4 * 4 + (col + shift) % 4


def along_x(col, shift):
    return (col + 4 * shift) % 16


def along_both(first, second, shift):
    return [
        (16 * row + col, 16 * row + (first, second)[row % 2](col, shift)) for row in range(8) for col in range(16)
    ]


OTHER_CORE = [(i, i ^ 1) for i in range(8)]
Y_BY_CORE = [(i, (i + 2 - 4 * (i % 2)) % 8) for i in range(8)]


def resident(value):
    return pltpu.with_memory_space_constraint(value, pltpu.VMEM)


def my_core():
    return lax.axis_index("row") % 2


def first_row(dy, dcore):
    index = lax.axis_index("row")
    y, core = index // 2, index % 2
    return pl.multiple_of((y + dy) % 4 * 2 * BLOCK + (core + dcore) % 2 * BLOCK, BLOCK)


def store_products(result, products, places, q, columns=slice(None)):
    for i, (dy, dcore) in enumerate(places):
        products[q, pl.ds(first_row(dy, dcore), BLOCK), columns] = result[i * BLOCK : (i + 1) * BLOCK]


def near_kernel(places, own, other, queries, products, held, token, rows, sems):
    nq, width, _ = held.shape
    half = width // 2
    chunks = [(0, slice(0, half)), (0, slice(half, width))]
    chunks += [(q, slice(0, width)) for q in range(1, nq - 1)]
    chunks += [(nq - 1, slice(0, half)), (nq - 1, slice(half, width))]
    copies = [
        pltpu.make_async_copy(queries.at[q, part], held.at[q, part], sems.at[i]) for i, (q, part) in enumerate(chunks)
    ]
    block_copies = [
        pltpu.make_async_copy(block, rows.at[pl.ds(i * BLOCK, BLOCK)], sems.at[len(copies) + i])
        for i, block in enumerate((own, other))
    ]
    for copy in block_copies + copies:
        copy.start()
    token[...] = jnp.zeros_like(token)
    for copy in block_copies:
        copy.wait()
    for copy, (q, part) in zip(copies, chunks, strict=True):
        copy.wait()
        result = lax.dot_general(rows[...], held[q, part], NT, preferred_element_type=jnp.float32)
        store_products(result, products, places, q, part)


def near_products(places, own, other, queries, tokens):
    nq, width, depth = queries.shape
    return pl.pallas_call(
        functools.partial(near_kernel, places),
        in_specs=[HBM, VMEM, HBM],
        out_specs=[VMEM] * 3,
        out_shape=[pltpu.VMEM((nq, tokens, width), jnp.float32), pltpu.VMEM(queries.shape, queries.dtype), TOKEN],
        scratch_shapes=[pltpu.VMEM((2 * BLOCK, depth), own.dtype), pltpu.SemaphoreType.DMA((2 * nq + 2,))],
        compiler_params=SMALL,
        cost_estimate=pl.CostEstimate(
            flops=WEIGHT * 4 * BLOCK * queries.size, bytes_accessed=2 * queries.size, transcendentals=0
        ),
        name="near",
    )(pltpu.with_memory_space_constraint(own, pltpu.HBM), other, queries)


def next_kernel(places, computed, rows, held, _, products, token):
    token[...] = jnp.zeros_like(token)
    for q in range(*computed):
        result = lax.dot_general(rows[...], held[q], NT, preferred_element_type=jnp.float32)
        store_products(result, products, places, q)


def next_products(name, places, rows, held, products, computed):
    share = computed[1] - computed[0]
    return pl.pallas_call(
        functools.partial(next_kernel, places, computed),
        in_specs=[VMEM] * 3,
        out_specs=[VMEM] * 2,
        out_shape=[pltpu.VMEM(products.shape, products.dtype), TOKEN],
        input_output_aliases={2: 0},
        compiler_params=SMALL,
        cost_estimate=pl.CostEstimate(
            flops=WEIGHT * share * rows.shape[0] * held.size // 2, bytes_accessed=2 * rows.size, transcendentals=0
        ),
        name=name,
    )(rows, resident(held), resident(products))


def pair_kernel(below, above, _, pair, onward):
    pair[:BLOCK, :] = below[...]
    pair[BLOCK:, :] = above[...]

    @pl.when(my_core() == 0)
    def _():
        onward[...] = below[...]

    @pl.when(my_core() == 1)
    def _():
        onward[...] = above[...]


def pair_up(below, above, token):
    rows, depth = below.shape
    return pl.pallas_call(
        pair_kernel,
        in_specs=[VMEM] * 3,
        out_specs=[VMEM] * 2,
        out_shape=[pltpu.VMEM((2 * rows, depth), below.dtype), pltpu.VMEM(below.shape, below.dtype)],
        compiler_params=SMALL,
        name="pair",
    )(below, above, token)


def stack_kernel(*refs):
    *blocks, _, out = refs
    for i, block in enumerate(blocks):
        out[i] = block[...]


def stack(blocks, token):
    return pl.pallas_call(
        stack_kernel,
        in_specs=[VMEM] * (len(blocks) + 1),
        out_specs=VMEM,
        out_shape=pltpu.VMEM((len(blocks),) + blocks[0].shape, blocks[0].dtype),
        compiler_params=SMALL,
        name="stack",
    )(*blocks, token)


def join_kernel(first, second, both):
    both[:BLOCK, :] = first[...]
    both[BLOCK:, :] = second[...]


def join(first, second):
    rows, depth = first.shape
    return pl.pallas_call(
        join_kernel,
        in_specs=[VMEM] * 2,
        out_specs=VMEM,
        out_shape=pltpu.VMEM((2 * rows, depth), first.dtype),
        compiler_params=SMALL,
        name="join",
    )(first, second)


def score_kernel(seq_start, seq_len, own, ahead, far, behind, products, out, lanes):
    col = lax.axis_index("col")
    x, z, core = col // 4, col % 4, my_core()
    nq = out.shape[0]
    width = products.shape[2]
    position = lax.broadcasted_iota(jnp.int32, (SLOT, 128), 0)
    for d, block in enumerate((own, ahead, far, behind)):

        def one_slot(i, carry, d=d, block=block):
            dx, dz = jnp.where(core == 0, d, i), jnp.where(core == 0, i, d)
            slot = (x + dx) % 4 * 4 + (z + dz) % 4
            base = pl.multiple_of(slot * SLOT, SLOT)
            token = position + base
            start = seq_start[slot]
            inside = (token >= start) & (token < start + seq_len[slot])
            totals = [jnp.zeros((SLOT, 128), jnp.float32) for _ in range(nq)]
            for w in range(0, width, 128):
                act = block[i, :, w : w + 128].astype(jnp.float32)
                for q in range(nq):
                    totals[q] += products[q, pl.ds(base, SLOT), w : w + 128] * act
            for q in range(nq):
                kept = jnp.where(inside, totals[q], 0.0)
                lanes[q, pl.ds(slot, 1), :] = jnp.sum(kept, axis=0, keepdims=True)
            return carry

        lax.fori_loop(0, 4, one_slot, 0)
    ones = jnp.ones((8, 128), jnp.float32)
    for q in range(nq):
        sums = lax.dot_general(ones, lanes[q], NT, precision=lax.Precision.HIGHEST, preferred_element_type=jnp.float32)
        out[q : q + 1, :] = sums[:1, :]


def partial_scores(seq_start, seq_len, acts, products):
    nq = products.shape[0]
    nseq = seq_start.shape[0]
    return pl.pallas_call(
        score_kernel,
        in_specs=[SMEM] * 2 + [VMEM] * (len(acts) + 1),
        out_specs=VMEM,
        out_shape=jax.ShapeDtypeStruct((nq, nseq), jnp.float32),
        scratch_shapes=[pltpu.VMEM((nq, nseq, 128), jnp.float32)],
        compiler_params=SMALL,
        cost_estimate=pl.CostEstimate(flops=1 << 30, bytes_accessed=4 << 20, transcendentals=0),
        name="scores",
    )(seq_start, seq_len, *acts, resident(products))


def from_all(value, axis):
    copies = jnp.broadcast_to(value[None], (lax.axis_size(axis),) + value.shape)
    return lax.all_to_all(copies, axis, 0, 0, tiled=True)


def on_device(activations, out_grads, queries, seq_start, seq_len):
    tokens = SLOT * seq_start.shape[0]
    nq = queries.shape[0]

    def to_core(block):
        return lax.ppermute(block, "row", OTHER_CORE)

    below = lax.ppermute(out_grads, "row", along_y(1))
    above = lax.ppermute(out_grads, "row", along_y(-1))
    other = to_core(out_grads)
    first_acts = [lax.ppermute(activations, ("row", "col"), along_both(along_z, along_x, -d)) for d in (1, 2, 3)]

    products, held, token = near_products([(0, 0), (0, 1)], out_grads, other, queries, tokens)
    own_act = stack([activations] + first_acts, token)
    acts = [own_act] + [lax.ppermute(own_act, ("row", "col"), along_both(along_x, along_z, -d)) for d in (1, 2, 3)]
    pair, onward = pair_up(below, above, token)
    pair_other = to_core(pair)
    far = lax.ppermute(onward, "row", Y_BY_CORE)

    products, token = next_products("mid", [(3, 0), (1, 0)], pair, held, products, (0, nq))
    places = [(3, 1), (1, 1)]
    products, token = next_products("other_low", places, pair_other, held, products, (0, nq // 2))
    (far,) = stack([far], token)
    far_other = to_core(far)
    products, token = next_products("other_high", places, pair_other, held, products, (nq // 2, nq))
    products, token = next_products("far", [(2, 0), (2, 1)], join(far, far_other), held, products, (0, nq))
    scores = partial_scores(seq_start, seq_len, acts, products)
    scores = jnp.sum(from_all(scores, "row"), axis=0)
    return jnp.sum(from_all(scores, "col"), axis=0)


def solution(mesh):
    in_specs = (P("col", "row"), P("row", "col"), P(None, "row", "col"), P(), P())
    return jax.shard_map(on_device, mesh=mesh, in_specs=in_specs, out_specs=P(), check_vma=False)
```

```python
import functools

import jax
import jax.numpy as jnp
from jax import lax
from jax.experimental import pallas as pl
from jax.experimental.pallas import tpu as pltpu
from jax.sharding import PartitionSpec as P

NT = (((1,), (1,)), ((), ()))
SLOT = 64
BLOCK = 128
VMEM = pl.BlockSpec(memory_space=pltpu.VMEM)
SMEM = pl.BlockSpec(memory_space=pltpu.SMEM)
HBM = pl.BlockSpec(memory_space=pltpu.HBM)
TOKEN = pltpu.VMEM((8, 128), jnp.float32)
SMALL = pltpu.CompilerParams(vmem_limit_bytes=8 << 20)
WEIGHT = 10


def along_y(shift):
    return [(i, ((i // 2 + shift) % 4) * 2 + i % 2) for i in range(8)]


def along_z(col, shift):
    return col // 4 * 4 + (col + shift) % 4


def along_x(col, shift):
    return (col + 4 * shift) % 16


def along_both(first, second, shift):
    return [
        (16 * row + col, 16 * row + (first, second)[row % 2](col, shift)) for row in range(8) for col in range(16)
    ]


OTHER_CORE = [(i, i ^ 1) for i in range(8)]
SAME_CORE = [[16 * row + col for row in range(core, 8, 2) for col in range(16)] for core in range(2)]
Y_BY_CORE = [(i, (i + 2 - 4 * (i % 2)) % 8) for i in range(8)]


def resident(value):
    return pltpu.with_memory_space_constraint(value, pltpu.VMEM)


def my_core():
    return lax.axis_index("row") % 2


def first_row(dy, dcore):
    index = lax.axis_index("row")
    y, core = index // 2, index % 2
    return pl.multiple_of((y + dy) % 4 * 2 * BLOCK + (core + dcore) % 2 * BLOCK, BLOCK)


def store_products(result, products, places, q, columns=slice(None)):
    for i, (dy, dcore) in enumerate(places):
        products[q, pl.ds(first_row(dy, dcore), BLOCK), columns] = result[i * BLOCK : (i + 1) * BLOCK]


def near_kernel(places, own, other, queries, products, held, token, rows, sems):
    nq, width, _ = held.shape
    half = width // 2
    chunks = [(0, slice(0, half)), (0, slice(half, width))]
    chunks += [(q, slice(0, width)) for q in range(1, nq - 1)]
    chunks += [(nq - 1, slice(0, half)), (nq - 1, slice(half, width))]
    copies = [
        pltpu.make_async_copy(queries.at[q, part], held.at[q, part], sems.at[i]) for i, (q, part) in enumerate(chunks)
    ]
    block_copies = [
        pltpu.make_async_copy(block, rows.at[pl.ds(i * BLOCK, BLOCK)], sems.at[len(copies) + i])
        for i, block in enumerate((own, other))
    ]
    for copy in block_copies + copies:
        copy.start()
    token[...] = jnp.zeros_like(token)
    for copy in block_copies:
        copy.wait()
    for copy, (q, part) in zip(copies, chunks, strict=True):
        copy.wait()
        result = lax.dot_general(rows[...], held[q, part], NT, preferred_element_type=jnp.float32)
        store_products(result, products, places, q, part)


def near_products(places, own, other, queries, tokens):
    nq, width, depth = queries.shape
    return pl.pallas_call(
        functools.partial(near_kernel, places),
        in_specs=[HBM, VMEM, HBM],
        out_specs=[VMEM] * 3,
        out_shape=[pltpu.VMEM((nq, tokens, width), jnp.float32), pltpu.VMEM(queries.shape, queries.dtype), TOKEN],
        scratch_shapes=[pltpu.VMEM((2 * BLOCK, depth), own.dtype), pltpu.SemaphoreType.DMA((2 * nq + 2,))],
        compiler_params=SMALL,
        cost_estimate=pl.CostEstimate(
            flops=WEIGHT * 4 * BLOCK * queries.size, bytes_accessed=2 * queries.size, transcendentals=0
        ),
        name="near",
    )(pltpu.with_memory_space_constraint(own, pltpu.HBM), other, queries)


def next_kernel(places, computed, rows, held, _, products, token):
    token[...] = jnp.zeros_like(token)
    for q in range(*computed):
        result = lax.dot_general(rows[...], held[q], NT, preferred_element_type=jnp.float32)
        store_products(result, products, places, q)


def next_products(name, places, rows, held, products, computed):
    share = computed[1] - computed[0]
    return pl.pallas_call(
        functools.partial(next_kernel, places, computed),
        in_specs=[VMEM] * 3,
        out_specs=[VMEM] * 2,
        out_shape=[pltpu.VMEM(products.shape, products.dtype), TOKEN],
        input_output_aliases={2: 0},
        compiler_params=SMALL,
        cost_estimate=pl.CostEstimate(
            flops=WEIGHT * share * rows.shape[0] * held.size // 2, bytes_accessed=2 * rows.size, transcendentals=0
        ),
        name=name,
    )(rows, resident(held), resident(products))


def pair_kernel(below, above, _, pair, onward):
    pair[:BLOCK, :] = below[...]
    pair[BLOCK:, :] = above[...]

    @pl.when(my_core() == 0)
    def _():
        onward[...] = below[...]

    @pl.when(my_core() == 1)
    def _():
        onward[...] = above[...]


def pair_up(below, above, token):
    rows, depth = below.shape
    return pl.pallas_call(
        pair_kernel,
        in_specs=[VMEM] * 3,
        out_specs=[VMEM] * 2,
        out_shape=[pltpu.VMEM((2 * rows, depth), below.dtype), pltpu.VMEM(below.shape, below.dtype)],
        compiler_params=SMALL,
        name="pair",
    )(below, above, token)


def stack_kernel(*refs):
    *blocks, _, out = refs
    for i, block in enumerate(blocks):
        out[i] = block[...]


def stack(blocks, token):
    return pl.pallas_call(
        stack_kernel,
        in_specs=[VMEM] * (len(blocks) + 1),
        out_specs=VMEM,
        out_shape=pltpu.VMEM((len(blocks),) + blocks[0].shape, blocks[0].dtype),
        compiler_params=SMALL,
        name="stack",
    )(*blocks, token)


def join_kernel(first, second, both):
    both[:BLOCK, :] = first[...]
    both[BLOCK:, :] = second[...]


def join(first, second):
    rows, depth = first.shape
    return pl.pallas_call(
        join_kernel,
        in_specs=[VMEM] * 2,
        out_specs=VMEM,
        out_shape=pltpu.VMEM((2 * rows, depth), first.dtype),
        compiler_params=SMALL,
        name="join",
    )(first, second)


def score_kernel(seq_start, seq_len, own, ahead, far, behind, products, out, lanes):
    col = lax.axis_index("col")
    x, z, core = col // 4, col % 4, my_core()
    nq = out.shape[0]
    width = products.shape[2]
    position = lax.broadcasted_iota(jnp.int32, (SLOT, 128), 0)
    for d, block in enumerate((own, ahead, far, behind)):

        def one_slot(i, carry, d=d, block=block):
            dx, dz = jnp.where(core == 0, d, i), jnp.where(core == 0, i, d)
            slot = (x + dx) % 4 * 4 + (z + dz) % 4
            base = pl.multiple_of(slot * SLOT, SLOT)
            token = position + base
            start = seq_start[slot]
            inside = (token >= start) & (token < start + seq_len[slot])
            totals = [jnp.zeros((SLOT, 128), jnp.float32) for _ in range(nq)]
            for w in range(0, width, 128):
                act = block[i, :, w : w + 128].astype(jnp.float32)
                for q in range(nq):
                    totals[q] += products[q, pl.ds(base, SLOT), w : w + 128] * act
            for q in range(nq):
                kept = jnp.where(inside, totals[q], 0.0)
                lanes[q, pl.ds(slot, 1), :] = jnp.sum(kept, axis=0, keepdims=True)
            return carry

        lax.fori_loop(0, 4, one_slot, 0)
    ones = jnp.ones((8, 128), jnp.float32)
    for q in range(nq):
        sums = lax.dot_general(ones, lanes[q], NT, precision=lax.Precision.HIGHEST, preferred_element_type=jnp.float32)
        out[q : q + 1, :] = sums[:1, :]


def partial_scores(seq_start, seq_len, acts, products):
    nq = products.shape[0]
    nseq = seq_start.shape[0]
    return pl.pallas_call(
        score_kernel,
        in_specs=[SMEM] * 2 + [VMEM] * (len(acts) + 1),
        out_specs=VMEM,
        out_shape=jax.ShapeDtypeStruct((nq, nseq), jnp.float32),
        scratch_shapes=[pltpu.VMEM((nq, nseq, 128), jnp.float32)],
        compiler_params=SMALL,
        cost_estimate=pl.CostEstimate(flops=1 << 30, bytes_accessed=4 << 20, transcendentals=0),
        name="scores",
    )(seq_start, seq_len, *acts, resident(products))


def total(value):
    value = value + lax.ppermute(value, "row", OTHER_CORE)
    copies = jnp.broadcast_to(value[None], (len(SAME_CORE[0]),) + value.shape)
    return jnp.sum(lax.all_to_all(copies, ("row", "col"), 0, 0, axis_index_groups=SAME_CORE, tiled=True), axis=0)


def on_device(activations, out_grads, queries, seq_start, seq_len):
    tokens = SLOT * seq_start.shape[0]
    nq = queries.shape[0]

    def to_core(block):
        return lax.ppermute(block, "row", OTHER_CORE)

    below = lax.ppermute(out_grads, "row", along_y(1))
    above = lax.ppermute(out_grads, "row", along_y(-1))
    other = to_core(out_grads)
    first_acts = [lax.ppermute(activations, ("row", "col"), along_both(along_z, along_x, -d)) for d in (1, 2, 3)]

    products, held, token = near_products([(0, 0), (0, 1)], out_grads, other, queries, tokens)
    own_act = stack([activations] + first_acts, token)
    acts = [own_act] + [lax.ppermute(own_act, ("row", "col"), along_both(along_x, along_z, -d)) for d in (1, 2, 3)]
    pair, onward = pair_up(below, above, token)
    pair_other = to_core(pair)
    far = lax.ppermute(onward, "row", Y_BY_CORE)

    products, token = next_products("mid", [(3, 0), (1, 0)], pair, held, products, (0, nq))
    places = [(3, 1), (1, 1)]
    products, token = next_products("other_low", places, pair_other, held, products, (0, nq // 2))
    (far,) = stack([far], token)
    far_other = to_core(far)
    products, token = next_products("other_high", places, pair_other, held, products, (nq // 2, nq))
    products, token = next_products("far", [(2, 0), (2, 1)], join(far, far_other), held, products, (0, nq))
    scores = partial_scores(seq_start, seq_len, acts, products)
    return total(scores)


def solution(mesh):
    in_specs = (P("col", "row"), P("row", "col"), P(None, "row", "col"), P(), P())
    return jax.shard_map(on_device, mesh=mesh, in_specs=in_specs, out_specs=P(), check_vma=False)
```

```python
import functools

import jax
import jax.numpy as jnp
from jax import lax
from jax.experimental import pallas as pl
from jax.experimental.pallas import tpu as pltpu
from jax.sharding import PartitionSpec as P

NT = (((1,), (1,)), ((), ()))
SLOT = 64
BLOCK = 128
PART = 16
VMEM = pl.BlockSpec(memory_space=pltpu.VMEM)
SMEM = pl.BlockSpec(memory_space=pltpu.SMEM)
HBM = pl.BlockSpec(memory_space=pltpu.HBM)
TOKEN = pltpu.VMEM((8, 128), jnp.float32)
SMALL = pltpu.CompilerParams(vmem_limit_bytes=8 << 20)
WEIGHT = 10


def along_y(shift):
    return [(i, ((i // 2 + shift) % 4) * 2 + i % 2) for i in range(8)]


def along_z(col, shift):
    return col // 4 * 4 + (col + shift) % 4


def along_x(col, shift):
    return (col + 4 * shift) % 16


def along_both(first, second, shift):
    return [
        (16 * row + col, 16 * row + (first, second)[row % 2](col, shift)) for row in range(8) for col in range(16)
    ]


OTHER_CORE = [(i, i ^ 1) for i in range(8)]
SAME_CORE = [[16 * row + col for row in range(core, 8, 2) for col in range(16)] for core in range(2)]
Y_BY_CORE = [(i, (i + 2 - 4 * (i % 2)) % 8) for i in range(8)]


def resident(value):
    return pltpu.with_memory_space_constraint(value, pltpu.VMEM)


def my_core():
    return lax.axis_index("row") % 2


def first_row(dy, dcore):
    index = lax.axis_index("row")
    y, core = index // 2, index % 2
    return pl.multiple_of((y + dy) % 4 * 2 * BLOCK + (core + dcore) % 2 * BLOCK, BLOCK)


def store_products(result, products, places, q):
    for i, (dy, dcore) in enumerate(places):
        products[q, pl.ds(first_row(dy, dcore), BLOCK), :] = result[i * BLOCK : (i + 1) * BLOCK]


def near_kernel(places, own, other, queries, products, held, token, rows, sems):
    copies = [pltpu.make_async_copy(queries.at[q], held.at[q], sems.at[q]) for q in range(held.shape[0])]
    block_copies = [
        pltpu.make_async_copy(block, rows.at[pl.ds(i * BLOCK, BLOCK)], sems.at[len(copies) + i])
        for i, block in enumerate((own, other))
    ]
    for copy in block_copies + copies:
        copy.start()
    token[...] = jnp.zeros_like(token)
    for copy in block_copies:
        copy.wait()
    for q, copy in enumerate(copies):
        copy.wait()
        result = lax.dot_general(rows[...], held[q], NT, preferred_element_type=jnp.float32)
        store_products(result, products, places, q)


def near_products(places, own, other, queries, tokens):
    nq, width, depth = queries.shape
    return pl.pallas_call(
        functools.partial(near_kernel, places),
        in_specs=[HBM, VMEM, HBM],
        out_specs=[VMEM] * 3,
        out_shape=[pltpu.VMEM((nq, tokens, width), jnp.float32), pltpu.VMEM(queries.shape, queries.dtype), TOKEN],
        scratch_shapes=[pltpu.VMEM((2 * BLOCK, depth), own.dtype), pltpu.SemaphoreType.DMA((nq + 2,))],
        compiler_params=SMALL,
        cost_estimate=pl.CostEstimate(
            flops=WEIGHT * 4 * BLOCK * queries.size, bytes_accessed=2 * queries.size, transcendentals=0
        ),
        name="near",
    )(pltpu.with_memory_space_constraint(own, pltpu.HBM), other, queries)


def next_kernel(places, computed, rows, held, _, products, token):
    token[...] = jnp.zeros_like(token)
    for q in range(*computed):
        result = lax.dot_general(rows[...], held[q], NT, preferred_element_type=jnp.float32)
        store_products(result, products, places, q)


def next_products(name, places, rows, held, products, computed):
    share = computed[1] - computed[0]
    return pl.pallas_call(
        functools.partial(next_kernel, places, computed),
        in_specs=[VMEM] * 3,
        out_specs=[VMEM] * 2,
        out_shape=[pltpu.VMEM(products.shape, products.dtype), TOKEN],
        input_output_aliases={2: 0},
        compiler_params=SMALL,
        cost_estimate=pl.CostEstimate(
            flops=WEIGHT * share * rows.shape[0] * held.size // 2, bytes_accessed=2 * rows.size, transcendentals=0
        ),
        name=name,
    )(rows, resident(held), resident(products))


def pair_kernel(below, above, _, pair, onward):
    pair[:BLOCK, :] = below[...]
    pair[BLOCK:, :] = above[...]

    @pl.when(my_core() == 0)
    def _():
        onward[...] = below[...]

    @pl.when(my_core() == 1)
    def _():
        onward[...] = above[...]


def pair_up(below, above, token):
    rows, depth = below.shape
    return pl.pallas_call(
        pair_kernel,
        in_specs=[VMEM] * 3,
        out_specs=[VMEM] * 2,
        out_shape=[pltpu.VMEM((2 * rows, depth), below.dtype), pltpu.VMEM(below.shape, below.dtype)],
        compiler_params=SMALL,
        name="pair",
    )(below, above, token)


def stack_kernel(*refs):
    *blocks, _, out = refs
    for i, block in enumerate(blocks):
        out[i] = block[...]


def stack(blocks, token):
    return pl.pallas_call(
        stack_kernel,
        in_specs=[VMEM] * (len(blocks) + 1),
        out_specs=VMEM,
        out_shape=pltpu.VMEM((len(blocks),) + blocks[0].shape, blocks[0].dtype),
        compiler_params=SMALL,
        name="stack",
    )(*blocks, token)


def join_kernel(first, second, both):
    both[:BLOCK, :] = first[...]
    both[BLOCK:, :] = second[...]


def join(first, second):
    rows, depth = first.shape
    return pl.pallas_call(
        join_kernel,
        in_specs=[VMEM] * 2,
        out_specs=VMEM,
        out_shape=pltpu.VMEM((2 * rows, depth), first.dtype),
        compiler_params=SMALL,
        name="join",
    )(first, second)


def score_kernel(seq_start, seq_len, own, ahead, far, behind, products, out, lanes):
    col = lax.axis_index("col")
    x, z, core = col // 4, col % 4, my_core()
    nq = products.shape[0]
    width = products.shape[2]
    position = lax.broadcasted_iota(jnp.int32, (SLOT, 128), 0)
    for d, block in enumerate((own, ahead, far, behind)):

        def one_slot(i, carry, d=d, block=block):
            dx, dz = jnp.where(core == 0, d, i), jnp.where(core == 0, i, d)
            slot = (x + dx) % 4 * 4 + (z + dz) % 4
            base = pl.multiple_of(slot * SLOT, SLOT)
            token = position + base
            start = seq_start[slot]
            inside = (token >= start) & (token < start + seq_len[slot])
            kept = [jnp.zeros((PART, 128), jnp.float32) for _ in range(nq)]
            for part in range(0, SLOT, PART):
                totals = [jnp.zeros((PART, 128), jnp.float32) for _ in range(nq)]
                for w in range(0, width, 128):
                    act = block[i, part : part + PART, w : w + 128].astype(jnp.float32)
                    for q in range(nq):
                        totals[q] += products[q, pl.ds(base + part, PART), w : w + 128] * act
                for q in range(nq):
                    kept[q] += jnp.where(inside[part : part + PART], totals[q], 0.0)
            for q in range(nq):
                lanes[q, pl.ds(slot, 1), :] = jnp.sum(kept[q], axis=0, keepdims=True)
            return carry

        lax.fori_loop(0, 4, one_slot, 0)
    ones = jnp.ones((8, 128), jnp.float32)
    rows = lanes[...].reshape(nq * lanes.shape[1], 128)
    sums = lax.dot_general(ones, rows, NT, precision=lax.Precision.HIGHEST, preferred_element_type=jnp.float32)
    out[...] = sums[:1, :]


def partial_scores(seq_start, seq_len, acts, products):
    nq = products.shape[0]
    nseq = seq_start.shape[0]
    return pl.pallas_call(
        score_kernel,
        in_specs=[SMEM] * 2 + [VMEM] * (len(acts) + 1),
        out_specs=VMEM,
        out_shape=jax.ShapeDtypeStruct((1, nq * nseq), jnp.float32),
        scratch_shapes=[pltpu.VMEM((nq, nseq, 128), jnp.float32)],
        compiler_params=SMALL,
        cost_estimate=pl.CostEstimate(flops=1 << 30, bytes_accessed=4 << 20, transcendentals=0),
        name="scores",
    )(seq_start, seq_len, *acts, resident(products))


def total(value):
    value = value + lax.ppermute(value, "row", OTHER_CORE)
    copies = jnp.broadcast_to(value[None], (len(SAME_CORE[0]),) + value.shape)
    return jnp.sum(lax.all_to_all(copies, ("row", "col"), 0, 0, axis_index_groups=SAME_CORE, tiled=True), axis=0)


def on_device(activations, out_grads, queries, seq_start, seq_len):
    tokens = SLOT * seq_start.shape[0]
    nq = queries.shape[0]

    def to_core(block):
        return lax.ppermute(block, "row", OTHER_CORE)

    below = lax.ppermute(out_grads, "row", along_y(1))
    above = lax.ppermute(out_grads, "row", along_y(-1))
    other = to_core(out_grads)
    first_acts = [lax.ppermute(activations, ("row", "col"), along_both(along_z, along_x, -d)) for d in (1, 2, 3)]

    products, held, token = near_products([(0, 0), (0, 1)], out_grads, other, queries, tokens)
    own_act = stack([activations] + first_acts, token)
    acts = [own_act] + [lax.ppermute(own_act, ("row", "col"), along_both(along_x, along_z, -d)) for d in (1, 2, 3)]
    pair, onward = pair_up(below, above, token)
    pair_other = to_core(pair)
    far = lax.ppermute(onward, "row", Y_BY_CORE)

    products, token = next_products("mid", [(3, 0), (1, 0)], pair, held, products, (0, nq))
    places = [(3, 1), (1, 1)]
    products, token = next_products("other_low", places, pair_other, held, products, (0, nq // 2))
    (far,) = stack([far], token)
    far_other = to_core(far)
    products, token = next_products("other_high", places, pair_other, held, products, (nq // 2, nq))
    products, token = next_products("far", [(2, 0), (2, 1)], join(far, far_other), held, products, (0, nq))
    scores = partial_scores(seq_start, seq_len, acts, products)
    return total(scores).reshape(queries.shape[0], seq_start.shape[0])


def solution(mesh):
    in_specs = (P("col", "row"), P("row", "col"), P(None, "row", "col"), P(), P())
    return jax.shard_map(on_device, mesh=mesh, in_specs=in_specs, out_specs=P(), check_vma=False)
```

```python
import functools

import jax
import jax.numpy as jnp
from jax import lax
from jax.experimental import pallas as pl
from jax.experimental.pallas import tpu as pltpu
from jax.sharding import PartitionSpec as P

NT = (((1,), (1,)), ((), ()))
SLOT = 64
BLOCK = 128
PART = 16
VMEM = pl.BlockSpec(memory_space=pltpu.VMEM)
SMEM = pl.BlockSpec(memory_space=pltpu.SMEM)
HBM = pl.BlockSpec(memory_space=pltpu.HBM)
TOKEN = pltpu.VMEM((8, 128), jnp.float32)
SMALL = pltpu.CompilerParams(vmem_limit_bytes=8 << 20)
WEIGHT = 10


def along_y(shift):
    return [(i, ((i // 2 + shift) % 4) * 2 + i % 2) for i in range(8)]


def along_z(col, shift):
    return col // 4 * 4 + (col + shift) % 4


def along_x(col, shift):
    return (col + 4 * shift) % 16


def along_both(first, second, shift):
    return [
        (16 * row + col, 16 * row + (first, second)[row % 2](col, shift)) for row in range(8) for col in range(16)
    ]


OTHER_CORE = [(i, i ^ 1) for i in range(8)]
SAME_CORE = [[16 * row + col for row in range(core, 8, 2) for col in range(16)] for core in range(2)]
Y_BY_CORE = [(i, (i + 2 - 4 * (i % 2)) % 8) for i in range(8)]


def resident(value):
    return pltpu.with_memory_space_constraint(value, pltpu.VMEM)


def my_core():
    return lax.axis_index("row") % 2


def first_row(dy, dcore):
    index = lax.axis_index("row")
    y, core = index // 2, index % 2
    return pl.multiple_of((y + dy) % 4 * 2 * BLOCK + (core + dcore) % 2 * BLOCK, BLOCK)


def store_products(result, products, places, q):
    for i, (dy, dcore) in enumerate(places):
        products[q, pl.ds(first_row(dy, dcore), BLOCK), :] = result[i * BLOCK : (i + 1) * BLOCK]


def near_kernel(places, own, other, queries, products, held, token, rows, sems):
    copies = [pltpu.make_async_copy(queries.at[q], held.at[q], sems.at[q]) for q in range(held.shape[0])]
    block_copies = [
        pltpu.make_async_copy(block, rows.at[pl.ds(i * BLOCK, BLOCK)], sems.at[len(copies) + i])
        for i, block in enumerate((own, other))
    ]
    for copy in block_copies + copies:
        copy.start()
    token[...] = jnp.zeros_like(token)
    for copy in block_copies:
        copy.wait()
    for q, copy in enumerate(copies):
        copy.wait()
        result = lax.dot_general(rows[...], held[q], NT, preferred_element_type=jnp.float32)
        store_products(result, products, places, q)


def near_products(places, own, other, queries, tokens):
    nq, width, depth = queries.shape
    return pl.pallas_call(
        functools.partial(near_kernel, places),
        in_specs=[HBM, VMEM, HBM],
        out_specs=[VMEM] * 3,
        out_shape=[pltpu.VMEM((nq, tokens, width), jnp.float32), pltpu.VMEM(queries.shape, queries.dtype), TOKEN],
        scratch_shapes=[pltpu.VMEM((2 * BLOCK, depth), own.dtype), pltpu.SemaphoreType.DMA((nq + 2,))],
        compiler_params=SMALL,
        cost_estimate=pl.CostEstimate(
            flops=WEIGHT * 4 * BLOCK * queries.size, bytes_accessed=2 * queries.size, transcendentals=0
        ),
        name="near",
    )(pltpu.with_memory_space_constraint(own, pltpu.HBM), other, queries)


def next_kernel(places, computed, rows, held, _, products, token):
    token[...] = jnp.zeros_like(token)
    for q in range(*computed):
        result = lax.dot_general(rows[...], held[q], NT, preferred_element_type=jnp.float32)
        store_products(result, products, places, q)


def next_products(name, places, rows, held, products, computed):
    share = computed[1] - computed[0]
    return pl.pallas_call(
        functools.partial(next_kernel, places, computed),
        in_specs=[VMEM] * 3,
        out_specs=[VMEM] * 2,
        out_shape=[pltpu.VMEM(products.shape, products.dtype), TOKEN],
        input_output_aliases={2: 0},
        compiler_params=SMALL,
        cost_estimate=pl.CostEstimate(
            flops=WEIGHT * share * rows.shape[0] * held.size // 2, bytes_accessed=2 * rows.size, transcendentals=0
        ),
        name=name,
    )(rows, resident(held), resident(products))


def pair_kernel(below, above, _, pair, onward):
    pair[:BLOCK, :] = below[...]
    pair[BLOCK:, :] = above[...]

    @pl.when(my_core() == 0)
    def _():
        onward[...] = below[...]

    @pl.when(my_core() == 1)
    def _():
        onward[...] = above[...]


def pair_up(below, above, token):
    rows, depth = below.shape
    return pl.pallas_call(
        pair_kernel,
        in_specs=[VMEM] * 3,
        out_specs=[VMEM] * 2,
        out_shape=[pltpu.VMEM((2 * rows, depth), below.dtype), pltpu.VMEM(below.shape, below.dtype)],
        compiler_params=SMALL,
        name="pair",
    )(below, above, token)


def stack_kernel(*refs):
    *blocks, _, out = refs
    for i, block in enumerate(blocks):
        out[i] = block[...]


def stack(blocks, token):
    return pl.pallas_call(
        stack_kernel,
        in_specs=[VMEM] * (len(blocks) + 1),
        out_specs=VMEM,
        out_shape=pltpu.VMEM((len(blocks),) + blocks[0].shape, blocks[0].dtype),
        compiler_params=SMALL,
        name="stack",
    )(*blocks, token)


def join_kernel(first, second, both):
    both[:BLOCK, :] = first[...]
    both[BLOCK:, :] = second[...]


def join(first, second):
    rows, depth = first.shape
    return pl.pallas_call(
        join_kernel,
        in_specs=[VMEM] * 2,
        out_specs=VMEM,
        out_shape=pltpu.VMEM((2 * rows, depth), first.dtype),
        compiler_params=SMALL,
        name="join",
    )(first, second)


def score_kernel(seq_start, seq_len, own, ahead, far, behind, products, out, lanes):
    col = lax.axis_index("col")
    x, z, core = col // 4, col % 4, my_core()
    nq = products.shape[0]
    width = products.shape[2]
    position = lax.broadcasted_iota(jnp.int32, (SLOT, 128), 0)
    for d, block in enumerate((own, ahead, far, behind)):

        def one_slot(i, carry, d=d, block=block):
            dx, dz = jnp.where(core == 0, d, i), jnp.where(core == 0, i, d)
            slot = (x + dx) % 4 * 4 + (z + dz) % 4
            base = pl.multiple_of(slot * SLOT, SLOT)
            token = position + base
            start = seq_start[slot]
            inside = (token >= start) & (token < start + seq_len[slot])
            kept = [jnp.zeros((PART, 128), jnp.float32) for _ in range(nq)]
            for part in range(0, SLOT, PART):
                totals = [jnp.zeros((PART, 128), jnp.float32) for _ in range(nq)]
                for w in range(0, width, 128):
                    act = block[i, part : part + PART, w : w + 128].astype(jnp.float32)
                    for q in range(nq):
                        totals[q] += products[q, pl.ds(base + part, PART), w : w + 128] * act
                for q in range(nq):
                    kept[q] += jnp.where(inside[part : part + PART], totals[q], 0.0)
            for q in range(nq):
                lanes[q, pl.ds(slot, 1), :] = jnp.sum(kept[q], axis=0, keepdims=True)
            return carry

        lax.fori_loop(0, 4, one_slot, 0)
    ones = jnp.ones((8, 128), jnp.float32)
    rows = lanes[...].reshape(nq * lanes.shape[1], 128)
    sums = lax.dot_general(ones, rows, NT, precision=lax.Precision.HIGHEST, preferred_element_type=jnp.float32)
    out[...] = sums[:1, :]


def partial_scores(seq_start, seq_len, acts, products):
    nq = products.shape[0]
    nseq = seq_start.shape[0]
    return pl.pallas_call(
        score_kernel,
        in_specs=[SMEM] * 2 + [VMEM] * (len(acts) + 1),
        out_specs=VMEM,
        out_shape=jax.ShapeDtypeStruct((1, nq * nseq), jnp.float32),
        scratch_shapes=[pltpu.VMEM((nq, nseq, 128), jnp.float32)],
        compiler_params=SMALL,
        cost_estimate=pl.CostEstimate(flops=1 << 30, bytes_accessed=4 << 20, transcendentals=0),
        name="scores",
    )(seq_start, seq_len, *acts, resident(products))


def total(value):
    value = value + lax.ppermute(value, "row", OTHER_CORE)
    copies = jnp.broadcast_to(value[None], (len(SAME_CORE[0]),) + value.shape)
    return jnp.sum(lax.all_to_all(copies, ("row", "col"), 0, 0, axis_index_groups=SAME_CORE, tiled=True), axis=0)


def on_device(activations, out_grads, queries, seq_start, seq_len):
    tokens = SLOT * seq_start.shape[0]
    nq = queries.shape[0]

    def to_core(block):
        return lax.ppermute(block, "row", OTHER_CORE)

    below = lax.ppermute(out_grads, "row", along_y(1))
    above = lax.ppermute(out_grads, "row", along_y(-1))
    other = to_core(out_grads)
    first_acts = [lax.ppermute(activations, ("row", "col"), along_both(along_z, along_x, -d)) for d in (1, 2, 3)]

    products, held, token = near_products([(0, 0), (0, 1)], out_grads, other, queries, tokens)
    own_act = stack([activations] + first_acts, token)
    acts = [own_act] + [lax.ppermute(own_act, ("row", "col"), along_both(along_x, along_z, -d)) for d in (1, 2, 3)]
    pair, onward = pair_up(below, above, token)
    pair_other = to_core(pair)
    far = lax.ppermute(onward, "row", Y_BY_CORE)

    products, token = next_products("mid", [(3, 0), (1, 0)], pair, held, products, (0, nq))
    places = [(3, 1), (1, 1)]
    products, token = next_products("other_low", places, pair_other, held, products, (0, nq - 1))
    (far,) = stack([far], token)
    far_other = to_core(far)
    products, token = next_products("other_high", places, pair_other, held, products, (nq - 1, nq))
    products, token = next_products("far", [(2, 0), (2, 1)], join(far, far_other), held, products, (0, nq))
    scores = partial_scores(seq_start, seq_len, acts, products)
    return total(scores).reshape(queries.shape[0], seq_start.shape[0])


def solution(mesh):
    in_specs = (P("col", "row"), P("row", "col"), P(None, "row", "col"), P(), P())
    return jax.shard_map(on_device, mesh=mesh, in_specs=in_specs, out_specs=P(), check_vma=False)
```
